32 devices in a mesh: grp: 2 (over y), seq: 4 (over z), head: 2 (over x), sub: 2 (over core).
Axes of the slice: x: 2, y: 2, z: 4, core: 2. Of those that a mesh axis runs over, the one named last changes fastest.
Arguments:
- queries: float32 [1536, 2048], P(('grp', 'seq'), ('head', 'sub')), parts along dimension 0, may hold values from -6 to 6
- keys: float32 [1536, 2048], P(('grp', 'seq'), ('head', 'sub')), parts along dimension 0, may hold values from -6 to 6
- values: float32 [1536, 2048], P(('grp', 'seq'), ('head', 'sub')), parts along dimension 0, may hold values from -40 to 40
- opt_queries: float32 [16, 64, 2048], P(('grp', 'seq'), None, ('head', 'sub')), parts along dimension 0, may hold values from -6 to 6
- opt_keys: float32 [16, 64, 2048], P(('grp', 'seq'), None, ('head', 'sub')), parts along dimension 0, may hold values from -6 to 6
- opt_values: float32 [16, 64, 2048], P(('grp', 'seq'), None, ('head', 'sub')), parts along dimension 0, may hold values from -40 to 40
- opt_offsets: int32 [16], P(('grp', 'seq')), parts along dimension 0, may hold values from 0 to 192
- opt_lengths: int32 [16], P(('grp', 'seq')), parts along dimension 0, may hold values from 1 to 64, 320 in all
- norm_gain: float32 [2048], P(('head', 'sub')), may hold values from 0.5 to 2
- out_weight: bfloat16 [2048, 4096], P(('head', 'sub')), may hold values from -0.125 to 0.125
Outputs:
- ctx_out: bfloat16 [1536, 4096], P(('grp', 'seq'), ('head', 'sub')), parts along dimension 0
- opt_out: bfloat16 [16, 64, 4096], P(('grp', 'seq'), None, ('head', 'sub')), parts along dimension 0
The draws below stay inside these ranges and needn't reach their ends.
There are 2 independent parts, one for each index of `grp`. The reference program is written for one: setup_inputs(seed, part) draws one part's arguments, and reference() takes and returns one part's arrays. A program takes and returns all parts, laid end to end along the dimension named above; an argument that names none is the same for every part. Nothing has to cross between parts.
Inputs may be any that keep to these rules, and one draw needn't show every extreme that they name: `opt_lengths`: within each scoring group the 8 lengths sum to 320, and the longest option of each group has exactly 64 tokens in every draw.
All inputs are finite; a program needn't handle non-finite values.
Results may differ from the reference program's by a relative error of at most 0.017.
Values may be sent and summed in bfloat16 or wider, within the bound.
No kernel may reach another device: no remote copies, remote signals or barrier semaphores. Data moves between devices by JAX's collectives and lax.ppermute only.
A program may use at most 64 MiB of HBM per device.

```python
import math
import jax
import jax.numpy as jnp
import numpy as np
from jax import lax

D = 4096
H = 16
DH = 128
TOK_DEV = 192
OPT_DEV = 2
OPT_LEN = 64
HD = 2048
CONTEXT = 768
OPTS = 8
N_SEQ = 4
N_HEAD = 2
N_SUB = 2


def scaled_values(key, shape):
    base_key, col_key, row_key = jax.random.split(key, 3)
    base = jnp.clip(jax.random.normal(base_key, shape, jnp.float32), -4.0, 4.0)
    col_scale = jnp.exp(jax.random.uniform(col_key, (shape[-1],), jnp.float32, 0.0, math.log(10.0)))
    row_scale = jnp.exp(jax.random.uniform(row_key, shape[:-1] + (1,), jnp.float32, 0.0, math.log(10.0)))
    return 0.1 * base * col_scale * row_scale


def draw_values(key, part):
    return scaled_values(jax.random.fold_in(key, 11), (CONTEXT, HD))


def draw_opt_values(key, part):
    return scaled_values(jax.random.fold_in(key, 23), (OPTS, OPT_LEN, HD))


def set_ends(array, own_key, low, largest):
    spot = [jax.random.randint(jax.random.fold_in(own_key, axis), (), 0, length) for axis, length in enumerate(array.shape)]
    main_axis = array.shape.index(max(array.shape))
    neighbour = spot[:main_axis] + [(spot[main_axis] + 1) % array.shape[main_axis]] + spot[main_axis + 1:]
    return array.at[tuple(spot)].set(low).at[tuple(neighbour)].set(largest)


def block_levels(key, extent, pieces, smallest, high):
    level, own = 1.0, jax.random.fold_in(key, 6)
    for axis_at, parts in pieces:
        heights = jnp.exp(jax.random.uniform(jax.random.fold_in(own, axis_at), (parts,), jnp.float32, smallest / len(pieces), high / len(pieces)))
        level = level * jnp.repeat(heights, extent[axis_at] // parts).reshape([-1 if axis == axis_at else 1 for axis in range(len(extent))])
    return level


def length_profile(amount, total, bound, skew):
    loads = [(1 << 20) // math.isqrt(grade ** skew) + 1 for grade in range(2, amount + 1)]
    rest, counts = total - bound - (amount - 1), [1] * (amount - 1)
    while rest > 0:
        movable = [i for i in range(amount - 1) if counts[i] < bound]
        whole, budget = sum([loads[i] for i in movable]), rest
        for i in movable:
            more = min(bound - counts[i], max(1, budget * loads[i] // whole), rest)
            counts[i] = counts[i] + more
            rest = rest - more
    return np.array([bound] + counts)


def ragged(key, amount, total, most, slope):
    if amount == 2:
        one = jax.random.randint(key, (), max(1, total - most), min(most, total - 1) + 1)
        return jnp.stack([one, total - one])
    tallies = jnp.asarray(length_profile(amount, total, most, slope), jnp.int32)
    twos = (amount - 1) // 2
    donor, taker = tallies[1:1 + 2 * twos:2], tallies[2:2 + 2 * twos:2]
    slack = jnp.minimum(donor - 1, most - taker)
    passed = jax.random.randint(jax.random.fold_in(key, 1), (twos,), 0, 1 << 20) % (slack + 1)
    tallies = tallies.at[1:1 + 2 * twos:2].set(donor - passed).at[2:2 + 2 * twos:2].set(taker + passed)
    return tallies[jax.random.permutation(jax.random.fold_in(key, 2), amount)]


def centred(key, shape, width, bound, pieces=(), kind=jnp.bfloat16):
    level = block_levels(key, shape, pieces, -0.22, 0.18) if pieces else 1.0
    values = jax.random.normal(key, shape, jnp.float32) * width * level
    return jnp.minimum(jnp.maximum(values, -bound), bound).astype(kind)


def setup_inputs(seed: int = 0, part: int = 0) -> dict:
    arg_keys = jax.random.split(jax.random.key(seed), 11)
    part_keys = jax.random.split(jax.random.fold_in(arg_keys[10], part), 11)
    queries = centred(part_keys[0], (CONTEXT, HD), 1.0, 6.0, ((0, 4), (1, 4)), jnp.float32)
    keys = centred(part_keys[1], (CONTEXT, HD), 1.0, 6.0, ((0, 4), (1, 4)), jnp.float32)
    values = draw_values(jax.random.fold_in(jax.random.fold_in(arg_keys[10], part), 71), part)
    opt_queries = centred(part_keys[3], (OPTS, OPT_LEN, HD), 1.0, 6.0, ((0, 4), (2, 4)), jnp.float32)
    opt_keys = centred(part_keys[4], (OPTS, OPT_LEN, HD), 1.0, 6.0, ((0, 4), (2, 4)), jnp.float32)
    opt_values = draw_opt_values(jax.random.fold_in(jax.random.fold_in(arg_keys[10], part), 71), part)
    opt_offsets = set_ends(jax.random.randint(part_keys[6], (OPTS,), 0, TOK_DEV + 1), jax.random.fold_in(part_keys[6], 1), 0, TOK_DEV).astype(jnp.int32)
    opt_lengths = ragged(part_keys[7], OPTS, OPTS * (OPT_LEN * 5 // 8), OPT_LEN, 1).astype(jnp.int32)
    norm_gain = jnp.clip(jnp.exp(math.log(2.0) - 1.3862944 * jax.random.uniform(arg_keys[8], (HD,), jnp.float32) ** block_levels(arg_keys[8], (HD,), ((0, 4),), -0.2, 0.2)), 0.5, 2.0)
    out_weight = centred(arg_keys[9], (HD, D), HD ** -0.5, 0.125, ((0, 4),))
    return {"queries": queries, "keys": keys, "values": values, "opt_queries": opt_queries, "opt_keys": opt_keys, "opt_values": opt_values, "opt_offsets": opt_offsets, "opt_lengths": opt_lengths, "norm_gain": norm_gain, "out_weight": out_weight}


norm_epsilon = 1e-05

def head_norm(attended, gain, mask):
    mean_square = lax.optimization_barrier(jnp.mean(attended * attended, axis=-1, keepdims=True))
    return (attended * lax.rsqrt(mean_square + norm_epsilon) * gain * mask).astype(jnp.bfloat16)

def project_groups(normed, weight_groups):
    groups = weight_groups.shape[0]
    flat = normed.reshape(normed.shape[0], groups, weight_groups.shape[1])
    partial_value = jnp.einsum('rgk,gkd->grd', flat.astype(jnp.float32), weight_groups.astype(jnp.float32), precision=lax.Precision.HIGHEST)
    partial_value = lax.optimization_barrier(partial_value.astype(jnp.bfloat16)).astype(jnp.float32)
    return lax.optimization_barrier(jnp.sum(partial_value, axis=0)).astype(jnp.bfloat16)

def reference(queries, keys, values, opt_queries, opt_keys, opt_values, opt_offsets, opt_lengths, norm_gain, out_weight):
    highest = lax.Precision.HIGHEST
    groups = N_HEAD * N_SUB
    query_blocks = queries.reshape(N_SEQ, TOK_DEV, H, DH)
    key_blocks = keys.reshape(N_SEQ, TOK_DEV, H, DH)
    value_blocks = values.reshape(N_SEQ, TOK_DEV, H, DH)
    states = jnp.einsum('cthd,cthe->chde', key_blocks, value_blocks, precision=highest)
    running = jnp.cumsum(states, axis=0)
    prefix = jnp.concatenate([jnp.zeros((1, H, DH, DH), jnp.float32), running[:-1]], axis=0)
    gain = norm_gain.reshape(H, DH)
    weight_groups = out_weight.reshape(groups, HD // groups, D)
    option_queries = opt_queries.reshape(N_SEQ, OPT_DEV, OPT_LEN, H, DH)
    option_keys = opt_keys.reshape(N_SEQ, OPT_DEV, OPT_LEN, H, DH)
    option_values = opt_values.reshape(N_SEQ, OPT_DEV, OPT_LEN, H, DH)
    offsets = opt_offsets.reshape(N_SEQ, OPT_DEV)
    lengths = opt_lengths.reshape(N_SEQ, OPT_DEV)
    positions = jnp.arange(TOK_DEV, dtype=jnp.int32)
    causal = (positions[:, None] >= positions[None, :]).astype(jnp.float32)
    slots = jnp.arange(OPT_LEN, dtype=jnp.int32)
    slot_causal = (slots[:, None] >= slots[None, :]).astype(jnp.float32)

    def one_block(inputs):
        block_q, block_k, block_v, block_prefix, opt_q, opt_k, opt_v, block_offsets, block_lengths = inputs
        inter = jnp.einsum('thd,hde->the', block_q, block_prefix, precision=highest)
        scores = jnp.einsum('thd,shd->hts', block_q, block_k, precision=highest) * causal[None]
        intra = jnp.einsum('hts,she->the', scores, block_v, precision=highest)
        context_normed = head_norm(inter + intra, gain, 1.0)
        context_rows = project_groups(context_normed.reshape(TOK_DEV, HD), weight_groups)
        before = (positions[None, :] < block_offsets[:, None]).astype(jnp.float32)
        local = jnp.einsum('ot,thd,the->ohde', before, block_k, block_v, precision=highest)
        opt_state = block_prefix[None] + local
        opt_inter = jnp.einsum('oihd,ohde->oihe', opt_q, opt_state, precision=highest)
        opt_scores = jnp.einsum('oihd,ojhd->ohij', opt_q, opt_k, precision=highest) * slot_causal[None, None]
        opt_intra = jnp.einsum('ohij,ojhe->oihe', opt_scores, opt_v, precision=highest)
        valid = (slots[None, :] < block_lengths[:, None]).astype(jnp.float32)
        opt_normed = head_norm(opt_inter + opt_intra, gain, valid[:, :, None, None])
        opt_rows = project_groups(opt_normed.reshape(OPT_DEV * OPT_LEN, HD), weight_groups)
        return (context_rows, opt_rows.reshape(OPT_DEV, OPT_LEN, D))
    context_out, option_out = lax.map(one_block, (query_blocks, key_blocks, value_blocks, prefix, option_queries, option_keys, option_values, offsets, lengths))
    return (context_out.reshape(CONTEXT, D), option_out.reshape(OPTS, OPT_LEN, D))
```

```python
import functools

import jax
import jax.numpy as jnp
from jax import lax
from jax.experimental import pallas as pl
from jax.experimental.pallas import tpu as pltpu
from jax.sharding import PartitionSpec as P

DH = 128
EPS = 1e-05
RADIX = 4
f32 = jnp.float32
bf16 = jnp.bfloat16
HIGHEST = lax.Precision.HIGHEST
VMEM_LIMIT = 40 * 1024 * 1024

VMEM = pl.BlockSpec(memory_space=pltpu.VMEM)
SMEM = pl.BlockSpec(memory_space=pltpu.SMEM)


def call(body, out_shape, specs, flops, nbytes, out_specs=None, **more):
    single = not isinstance(out_shape, (tuple, list))
    if out_specs is None:
        out_specs = VMEM if single else [VMEM] * len(out_shape)
    return pl.pallas_call(
        body,
        out_shape=out_shape,
        in_specs=specs,
        out_specs=out_specs,
        compiler_params=pltpu.CompilerParams(vmem_limit_bytes=VMEM_LIMIT),
        cost_estimate=pl.CostEstimate(flops=flops, bytes_accessed=nbytes, transcendentals=0),
        **more,
    )


def states_kernel(k_ref, v_ref, out_ref):
    for h in range(out_ref.shape[0]):
        cols = slice(h * DH, (h + 1) * DH)
        out_ref[h] = lax.dot_general(
            k_ref[:, cols], v_ref[:, cols], (((0,), (0,)), ((), ())),
            precision=HIGHEST, preferred_element_type=f32,
        ).astype(out_ref.dtype)


def joined(ctx_ref, opt_ref, cols):
    return jnp.concatenate([ctx_ref[:, cols]] + [opt_ref[o, :, cols] for o in range(opt_ref.shape[0])], axis=0)


def base_kernel(offsets_ref, q_ref, k_ref, v_ref, oq_ref, ok_ref, ov_ref, out_ref):
    tokens, opts, slots = q_ref.shape[0], oq_ref.shape[0], oq_ref.shape[1]
    rows = tokens + opts * slots
    i = lax.broadcasted_iota(jnp.int32, (rows, rows), 0)
    j = lax.broadcasted_iota(jnp.int32, (rows, rows), 1)
    limit, first = i + 1, jnp.full((rows, rows), rows, jnp.int32)
    for o in range(opts):
        own = i >= tokens + o * slots
        limit = jnp.where(own, offsets_ref[o], limit)
        first = jnp.where(own, tokens + o * slots, first)
    mask = (j < limit) | ((j >= first) & (j <= i))
    for h in range(q_ref.shape[1] // DH):
        cols = slice(h * DH, (h + 1) * DH)
        q, k, v = joined(q_ref, oq_ref, cols), joined(k_ref, ok_ref, cols), joined(v_ref, ov_ref, cols)
        scores = lax.dot_general(q, k, (((1,), (1,)), ((), ())), precision=HIGHEST, preferred_element_type=f32)
        scores = jnp.where(mask, scores, 0.0)
        out_ref[:, cols] = jnp.dot(scores, v, precision=HIGHEST, preferred_element_type=f32)


def normed_kernel(shifts, place_ref, lengths_ref, q_ref, oq_ref, base_ref, gain_ref, *rest):
    parts, out_ref = rest[:-1], rest[-1]
    tokens, opts, slots = q_ref.shape[0], oq_ref.shape[0], oq_ref.shape[1]
    place = place_ref[0]
    row = lax.broadcasted_iota(jnp.int32, (tokens + opts * slots, 1), 0)
    valid = row < tokens
    for o in range(opts):
        start = tokens + o * slots
        valid = valid | ((row >= start) & (row < start + lengths_ref[o]))
    for h in range(q_ref.shape[1] // DH):
        cols = slice(h * DH, (h + 1) * DH)
        prefix = jnp.zeros((DH, DH), f32)
        for shift, part in zip(shifts, parts):
            prefix = prefix + jnp.where(place >= shift, part[h].astype(f32), 0.0)
        rows = base_ref[:, cols] + jnp.dot(
            joined(q_ref, oq_ref, cols), prefix, precision=HIGHEST, preferred_element_type=f32
        )
        scale = lax.rsqrt(jnp.mean(rows * rows, axis=1, keepdims=True) + EPS)
        out = rows * scale * gain_ref[:, cols]
        out_ref[:, cols] = jnp.where(valid, out, 0.0).astype(out_ref.dtype)


def project_kernel(*refs):
    half = (len(refs) - 1) // 2
    out_ref = refs[-1]
    total = jnp.dot(refs[0][...], refs[half][...], preferred_element_type=f32)
    for a, w in zip(refs[1:half], refs[half + 1:-1]):
        total = total + jnp.dot(a[...], w[...], preferred_element_type=f32)
    out_ref[...] = total.astype(out_ref.dtype)


def project(normeds, weights, dtype):
    rows, depth = normeds[0].shape
    width = weights[0].shape[1]
    n = len(normeds)
    return call(
        project_kernel, jax.ShapeDtypeStruct((rows, width), dtype), [VMEM] * (2 * n),
        2 * n * rows * depth * width, 2 * n * depth * (rows + width),
    )(*normeds, *weights)


def final_kernel(own_ref, *rest):
    parts, ctx_ref, opt_ref = rest[:-2], rest[-2], rest[-1]
    tokens, (opts, slots, width) = ctx_ref.shape[0], opt_ref.shape
    step = parts[0].shape[1]
    per = width // step
    for c in range(per):
        cols = slice(c * step, (c + 1) * step)
        total = own_ref[:, cols]
        for part in parts[c::per]:
            total = total + part[...].astype(f32)
        total = total.astype(ctx_ref.dtype)
        ctx_ref[:, cols] = total[:tokens]
        for o in range(opts):
            opt_ref[o, :, cols] = total[tokens + o * slots:tokens + (o + 1) * slots]


def ring(value, axis, size, shift):
    return lax.ppermute(value, axis, [(i, (i + shift) % size) for i in range(size)])


def on_device(sizes, q, k, v, oq, ok, ov, offsets, lengths, gain, weight):
    n_seq, n_head, n_sub = sizes
    tokens, feats = q.shape
    opts, slots, _ = oq.shape
    rows = tokens + opts * slots
    heads = feats // DH
    width = weight.shape[1] // (n_head * n_sub)
    place = lax.axis_index("seq")
    head, sub = lax.axis_index("head"), lax.axis_index("sub")

    state = call(
        states_kernel, jax.ShapeDtypeStruct((heads, DH, DH), bf16), [VMEM, VMEM],
        2 * tokens * DH * feats, 8 * tokens * feats,
    )(k, v)

    shifts, parts, window, step = [], [], state, 1
    while step < n_seq:
        now = [s for s in range(step, min(RADIX * step, n_seq), step)]
        got = [ring(window, "seq", n_seq, s) for s in now]
        shifts, parts = shifts + now, parts + got
        step *= RADIX
        if step < n_seq:
            add = window.astype(f32)
            for s, g in zip(now, got):
                add = add + jnp.where(place >= s, g.astype(f32), 0.0)
            window = add.astype(bf16)

    base = call(
        base_kernel, jax.ShapeDtypeStruct((rows, feats), f32), [SMEM] + [VMEM] * 6,
        4 * rows * rows * feats, 16 * rows * feats,
    )(offsets, q, k, v, oq, ok, ov)

    def columns(h, s):
        return lax.dynamic_slice_in_dim(weight, (h * n_sub + s) * width, width, 1)

    targets = [(head + d) % n_head for d in range(n_head)]
    weights = []
    for h in targets:
        ws = [columns(h, sub)]
        for d in range(1, n_sub):
            ws.append(ring(columns(h, (sub + d) % n_sub), "sub", n_sub, d))
        weights.append(ws)

    normed = call(
        functools.partial(normed_kernel, tuple(shifts)), jax.ShapeDtypeStruct((rows, feats), bf16),
        [SMEM, SMEM] + [VMEM] * (4 + len(parts)), 2 * rows * DH * feats, 10 * rows * feats,
    )(place[None], lengths, q, oq, base, gain[None], *parts)
    normeds = [normed] + [ring(normed, "sub", n_sub, d) for d in range(1, n_sub)]

    pieces = 4
    step = width // pieces
    received = []
    for d in range(1, n_head):
        for c in range(pieces):
            out = project(normeds, [w[:, c * step:(c + 1) * step] for w in weights[d]], bf16)
            received.append(ring(out, "head", n_head, d))
    own = project(normeds, weights[0], f32)
    ctx, opt = call(
        final_kernel,
        (jax.ShapeDtypeStruct((tokens, width), bf16), jax.ShapeDtypeStruct((opts, slots, width), bf16)),
        [VMEM] * (1 + len(received)), rows * width, 8 * rows * width,
    )(own, *received)
    return ctx, opt


def solution(mesh):
    placed = (
        P(("grp", "seq"), ("head", "sub")),
        P(("grp", "seq"), ("head", "sub")),
        P(("grp", "seq"), ("head", "sub")),
        P(("grp", "seq"), None, ("head", "sub")),
        P(("grp", "seq"), None, ("head", "sub")),
        P(("grp", "seq"), None, ("head", "sub")),
        P(("grp", "seq")),
        P(("grp", "seq")),
        P(("head", "sub")),
        P(("head", "sub"), None),
    )
    sizes = tuple(mesh.shape[a] for a in ("seq", "head", "sub"))
    return jax.shard_map(
        functools.partial(on_device, sizes),
        mesh=mesh,
        in_specs=placed,
        out_specs=(P(("grp", "seq"), ("head", "sub")), P(("grp", "seq"), None, ("head", "sub"))),
        check_vma=False,
    )
```

```python
import functools

import jax
import jax.numpy as jnp
from jax import lax
from jax.experimental import pallas as pl
from jax.experimental.pallas import tpu as pltpu
from jax.sharding import PartitionSpec as P

DH = 128
EPS = 1e-05
SPANS = ((0, 2), (2, 3), (3, 4))
f32 = jnp.float32
bf16 = jnp.bfloat16
HIGHEST = lax.Precision.HIGHEST
VMEM_LIMIT = 32 * 1024 * 1024

VMEM = pl.BlockSpec(memory_space=pltpu.VMEM)
SMEM = pl.BlockSpec(memory_space=pltpu.SMEM)
HBM = pl.BlockSpec(memory_space=pltpu.HBM)
ANY = pl.BlockSpec(memory_space=pl.ANY)
Shape = jax.ShapeDtypeStruct


def call(body, out_shape, specs, flops, nbytes, out_specs=None, limit=VMEM_LIMIT, **more):
    single = not isinstance(out_shape, (tuple, list))
    if out_specs is None:
        out_specs = VMEM if single else [VMEM] * len(out_shape)
    return pl.pallas_call(
        body,
        out_shape=out_shape,
        in_specs=specs,
        out_specs=out_specs,
        compiler_params=pltpu.CompilerParams(vmem_limit_bytes=limit),
        cost_estimate=pl.CostEstimate(flops=flops, bytes_accessed=nbytes, transcendentals=0),
        **more,
    )


def columns(h):
    return slice(h * DH, (h + 1) * DH)


def halves(x):
    high = x.astype(bf16)
    return high, (x - high.astype(f32)).astype(bf16)


def dot3(a, b, dims):
    (ah, al), (bh, bl) = a, b
    dot = functools.partial(lax.dot_general, dimension_numbers=(dims, ((), ())), preferred_element_type=f32)
    return dot(ah, bh) + (dot(ah, bl) + dot(al, bh))


def base_kernel(tokens, offsets_ref, qh, ql, kh, kl, vh, vl, after_ref, out_ref):
    rows, opts = out_ref.shape[0], offsets_ref.shape[0]
    slots = (rows - tokens) // opts
    i = lax.broadcasted_iota(jnp.int32, (rows, rows), 0)
    j = lax.broadcasted_iota(jnp.int32, (rows, rows), 1)
    limit, first = i + 1, jnp.full((rows, rows), rows, jnp.int32)
    for o in range(opts):
        own = i >= tokens + o * slots
        limit = jnp.where(own, offsets_ref[o], limit)
        first = jnp.where(own, tokens + o * slots, first)
    mask = (j < limit) | ((j >= first) & (j <= i))
    for h in range(out_ref.shape[1] // DH):
        cols = columns(h)
        scores = dot3((qh[:, cols], ql[:, cols]), (kh[:, cols], kl[:, cols]), ((1,), (1,)))
        scores = halves(jnp.where(mask, scores, 0.0))
        out_ref[:, cols] = dot3(scores, (vh[:, cols], vl[:, cols]), ((1,), (0,)))


def add_kernel(*refs):
    total = refs[0][...].astype(f32)
    for ref in refs[1:-1]:
        total = total + ref[...].astype(f32)
    refs[-1][...] = total.astype(refs[-1].dtype)


def add(*terms):
    return call(
        add_kernel, Shape(terms[0].shape, bf16), [VMEM] * len(terms),
        len(terms) * terms[0].size, 6 * len(terms) * terms[0].size,
    )(*terms)


def normed_kernel(tokens, use_ref, lengths_ref, qh, ql, base_ref, gain_ref, *rest):
    parts, out_ref = rest[:-1], rest[-1]
    (rows, feats), opts = out_ref.shape, lengths_ref.shape[0]
    slots = (rows - tokens) // opts
    row = lax.broadcasted_iota(jnp.int32, (rows, 1), 0)
    valid = row < tokens
    for o in range(opts):
        start = tokens + o * slots
        valid = valid | ((row >= start) & (row < start + lengths_ref[o]))
    for h in range(feats // DH):
        prefix = jnp.zeros((DH, DH), f32)
        for n, part in enumerate(parts):
            prefix = prefix + jnp.where(use_ref[n] > 0, part[h].astype(f32), 0.0)
        cols = columns(h)
        out = base_ref[:, cols] + dot3((qh[:, cols], ql[:, cols]), halves(prefix), ((1,), (0,)))
        scale = lax.rsqrt(jnp.mean(out * out, axis=1, keepdims=True) + EPS)
        out_ref[:, cols] = jnp.where(valid, out * scale * gain_ref[:, cols], 0.0).astype(out_ref.dtype)


def project_kernel(spans, rows_ref, weight_ref, *outs):
    for (start, end), out in zip(spans, outs):
        out[...] = jnp.dot(rows_ref[...], weight_ref[:, start:end], preferred_element_type=f32).astype(out.dtype)


def project(rows, weight, spans, dtype):
    count, (depth, width) = rows.shape[0], weight.shape
    return call(
        functools.partial(project_kernel, spans), [Shape((count, b - a), dtype) for a, b in spans], [VMEM] * 2,
        2 * count * depth * width, 2 * depth * (count + width) + 4 * count * width,
    )(rows, weight)


def final_kernel(spans, per, *rest):
    terms, (ctx_ref, opt_ref, buf, sem) = rest[:per * len(spans)], rest[-4:]
    tokens, (opts, slots, width) = ctx_ref.shape[0], opt_ref.shape
    low, high = spans[0][0], spans[-1][1]
    for c, (start, end) in enumerate(spans):
        total = terms[c * per][...].astype(f32)
        for term in terms[c * per + 1:(c + 1) * per]:
            total = total + term[...].astype(f32)
        buf[:, start - low:end - low] = total.astype(buf.dtype)
    copies = [pltpu.make_async_copy(buf.at[:tokens], ctx_ref.at[:, low:high], sem.at[0])]
    for o in range(opts):
        start = tokens + o * slots
        copies.append(pltpu.make_async_copy(buf.at[start:start + slots], opt_ref.at[o, :, low:high], sem.at[o + 1]))
    for copy in copies:
        copy.start()
    for copy in copies:
        copy.wait()


def final(spans, terms, shapes, before=()):
    flat = sum(terms, [])
    rows, width, opts, n = flat[0].shape[0], spans[-1][1] - spans[0][0], shapes[1].shape[0], len(flat)
    return call(
        functools.partial(final_kernel, spans, len(terms[0])), shapes, [VMEM] * n + [HBM] * len(before),
        rows * width * n, 4 * rows * width * n, out_specs=[HBM, HBM],
        input_output_aliases={n: 0, n + 1: 1} if before else {},
        scratch_shapes=[pltpu.VMEM((rows, width), bf16), pltpu.SemaphoreType.DMA((1 + opts,))],
    )(*flat, *before)


def ring(value, axis, size, shift):
    return lax.ppermute(value, axis, [(i, (i + shift) % size) for i in range(size)])


def swap(value, axis, size, mask):
    return lax.ppermute(value, axis, [(i, i ^ mask) for i in range(size)])


def exclusive(state, axis, size):
    place = lax.axis_index(axis)
    parts, use, windows, step = [], [], [state], 1
    while step < size:
        parts.append(swap(windows[-1], axis, size, step))
        use.append(place & step != 0)
        step *= 2
        if step < size:
            windows.append(add(windows[-1], parts[-1]))
    return parts, jnp.stack(use).astype(jnp.int32), windows[:2][-1]


def on_device(sizes, q, k, v, oq, ok, ov, offsets, lengths, gain, weight):
    n_seq, n_head, n_sub = sizes
    tokens, feats = q.shape
    opts, slots, _ = oq.shape
    rows = tokens + opts * slots
    heads = feats // DH
    width = weight.shape[1] // (n_head * n_sub)
    head, sub = lax.axis_index("head"), lax.axis_index("sub")

    state = jnp.einsum(
        "thd,the->hde", k.reshape(tokens, heads, DH), v.reshape(tokens, heads, DH), precision=lax.Precision.DEFAULT
    ).astype(bf16)
    parts, use, window = exclusive(state, "seq", n_seq)

    q, k, v, oq, ok, ov, _ = lax.optimization_barrier((q, k, v, oq, ok, ov, state))
    halved = [halves(jnp.concatenate([x, y.reshape(-1, feats)])) for x, y in ((q, oq), (k, ok), (v, ov))]
    base = call(
        functools.partial(base_kernel, tokens), Shape((rows, feats), f32), [SMEM] + [VMEM] * 6 + [ANY],
        12 * rows * rows * feats, 16 * rows * feats,
    )(offsets, *sum(halved, ()), window)
    normed = call(
        functools.partial(normed_kernel, tokens), Shape((rows, feats), bf16),
        [SMEM, SMEM] + [VMEM] * (4 + len(parts)), 6 * rows * DH * feats, 10 * rows * feats,
    )(use, lengths, *halved[0], base, gain[None], *parts)

    def blocks(d):
        at = [((head + d) % n_head * n_sub + (sub + s) % n_sub) * width for s in range(n_sub)]
        return [lax.dynamic_slice_in_dim(later, x, width, 1) for x in at]

    def summed(d, spans):
        ours, *theirs = weights[d]
        theirs = [project(normed, w, spans, bf16) for w in theirs]
        ours = project(normed, ours, spans, f32)
        theirs = [[ring(x, "sub", n_sub, s + 1) for x in xs] for s, xs in enumerate(theirs)]
        return list(zip(ours, *theirs))

    later, _ = lax.optimization_barrier((weight, window))
    weights = [blocks(d) for d in range(n_head)]
    spans = [(width * a // 4, width * b // 4) for a, b in SPANS]
    received = {}
    for d in range(1, n_head):
        for span, terms in zip(spans, summed(d, spans)):
            received[d, span] = ring(add(*terms), "head", n_head, d)
    own = dict(zip(spans, summed(0, spans)))
    shapes = (Shape((tokens, width), bf16), Shape((opts, slots, width), bf16))
    out = ()
    for some in (spans[:-1], spans[-1:]):
        terms = [[*own[span]] + [received[d, span] for d in range(1, n_head)] for span in some]
        out = final(some, terms, shapes, out)
    return tuple(out)


def solution(mesh):
    placed = (
        P(("grp", "seq"), ("head", "sub")),
        P(("grp", "seq"), ("head", "sub")),
        P(("grp", "seq"), ("head", "sub")),
        P(("grp", "seq"), None, ("head", "sub")),
        P(("grp", "seq"), None, ("head", "sub")),
        P(("grp", "seq"), None, ("head", "sub")),
        P(("grp", "seq")),
        P(("grp", "seq")),
        P(("head", "sub")),
        P(("head", "sub"), None),
    )
    sizes = tuple(mesh.shape[a] for a in ("seq", "head", "sub"))
    return jax.shard_map(
        functools.partial(on_device, sizes),
        mesh=mesh,
        in_specs=placed,
        out_specs=(P(("grp", "seq"), ("head", "sub")), P(("grp", "seq"), None, ("head", "sub"))),
        check_vma=False,
    )
```

```python
import functools

import jax
import jax.numpy as jnp
from jax import lax
from jax.experimental import pallas as pl
from jax.experimental.pallas import tpu as pltpu
from jax.sharding import PartitionSpec as P

DH = 128
EPS = 1e-05
SPANS = ((0, 2), (2, 3), (3, 4))
f32 = jnp.float32
bf16 = jnp.bfloat16
HIGHEST = lax.Precision.HIGHEST
VMEM_LIMIT = 32 * 1024 * 1024

VMEM = pl.BlockSpec(memory_space=pltpu.VMEM)
SMEM = pl.BlockSpec(memory_space=pltpu.SMEM)
HBM = pl.BlockSpec(memory_space=pltpu.HBM)
ANY = pl.BlockSpec(memory_space=pl.ANY)
Shape = jax.ShapeDtypeStruct


def call(body, out_shape, specs, flops, nbytes, out_specs=None, limit=VMEM_LIMIT, **more):
    single = not isinstance(out_shape, (tuple, list))
    if out_specs is None:
        out_specs = VMEM if single else [VMEM] * len(out_shape)
    return pl.pallas_call(
        body,
        out_shape=out_shape,
        in_specs=specs,
        out_specs=out_specs,
        compiler_params=pltpu.CompilerParams(vmem_limit_bytes=limit),
        cost_estimate=pl.CostEstimate(flops=flops, bytes_accessed=nbytes, transcendentals=0),
        **more,
    )


def columns(h):
    return slice(h * DH, (h + 1) * DH)


def halves(x):
    high = x.astype(bf16)
    return high, (x - high.astype(f32)).astype(bf16)


def dot3(a, b, dims):
    (ah, al), (bh, bl) = a, b
    dot = functools.partial(lax.dot_general, dimension_numbers=(dims, ((), ())), preferred_element_type=f32)
    return dot(ah, bh) + (dot(ah, bl) + dot(al, bh))


def joined(ctx_ref, opt_ref, cols):
    return jnp.concatenate([ctx_ref[:, cols]] + [opt_ref[o, :, cols] for o in range(opt_ref.shape[0])], axis=0)


def base_kernel(
    offsets_ref, lengths_ref, gain_ref, q_ref, k_ref, v_ref, oq_ref, ok_ref, ov_ref, after_ref, out_ref, qh_ref, ql_ref, gains_ref
):
    tokens, (opts, slots, _) = q_ref.shape[0], oq_ref.shape
    rows = tokens + opts * slots
    i = lax.broadcasted_iota(jnp.int32, (rows, rows), 0)
    j = lax.broadcasted_iota(jnp.int32, (rows, rows), 1)
    limit, first = i + 1, jnp.full((rows, rows), rows, jnp.int32)
    for o in range(opts):
        own = i >= tokens + o * slots
        limit = jnp.where(own, offsets_ref[o], limit)
        first = jnp.where(own, tokens + o * slots, first)
    row = lax.broadcasted_iota(jnp.int32, (rows, 1), 0)
    valid = row < tokens
    for o in range(opts):
        start = tokens + o * slots
        valid = valid | ((row >= start) & (row < start + lengths_ref[o]))
    gains_ref[...] = jnp.where(valid, gain_ref[...], 0.0)
    mask = (j < limit) | ((j >= first) & (j <= i))
    for h in range(out_ref.shape[1] // DH):
        cols = columns(h)
        q, k, v = (halves(joined(c, o, cols)) for c, o in ((q_ref, oq_ref), (k_ref, ok_ref), (v_ref, ov_ref)))
        qh_ref[:, cols], ql_ref[:, cols] = q
        scores = halves(jnp.where(mask, dot3(q, k, ((1,), (1,))), 0.0))
        out_ref[:, cols] = dot3(scores, v, ((1,), (0,)))


def add_kernel(*refs):
    out_ref = refs[-1]
    total = refs[0][:out_ref.shape[0]].astype(f32)
    for ref in refs[1:-1]:
        total = total + ref[:out_ref.shape[0]].astype(f32)
    out_ref[...] = total.astype(out_ref.dtype)


def add(*terms, rows=None):
    shape = (rows or terms[0].shape[0],) + terms[0].shape[1:]
    return call(
        add_kernel, Shape(shape, bf16), [VMEM] * len(terms), len(terms) * terms[0].size, 6 * len(terms) * terms[0].size,
    )(*terms)


def normed_kernel(spans, use_ref, qh, ql, base_ref, gains_ref, *rest):
    parts, out_ref = rest[:-1], rest[-1]
    for h in range(out_ref.shape[1] // DH):
        prefix = jnp.zeros((DH, DH), f32)
        for n, (low, high) in enumerate(spans):
            if low <= h < high:
                prefix = prefix + jnp.where(use_ref[n:n + 1] > 0.0, parts[n][h - low].astype(f32), 0.0)
        cols = columns(h)
        out = base_ref[:, cols] + dot3((qh[:, cols], ql[:, cols]), halves(prefix), ((1,), (0,)))
        scale = lax.rsqrt(jnp.mean(out * out, axis=1, keepdims=True) + EPS)
        out_ref[:, cols] = (out * scale * gains_ref[:, cols]).astype(out_ref.dtype)


def project_kernel(spans, rows_ref, weight_ref, *outs):
    for (start, end), out in zip(spans, outs):
        out[...] = jnp.dot(rows_ref[...], weight_ref[:, start:end], preferred_element_type=f32).astype(out.dtype)


def project(rows, weight, spans, dtype):
    count, (depth, width) = rows.shape[0], weight.shape
    return call(
        functools.partial(project_kernel, spans), [Shape((count, b - a), dtype) for a, b in spans], [VMEM] * 2,
        2 * count * depth * width, 2 * depth * (count + width) + 4 * count * width,
    )(rows, weight)


def final_kernel(spans, per, *rest):
    terms, (ctx_ref, opt_ref, buf, sem) = rest[:per * len(spans)], rest[-4:]
    tokens, (opts, slots, width) = ctx_ref.shape[0], opt_ref.shape
    low, high = spans[0][0], spans[-1][1]
    for c, (start, end) in enumerate(spans):
        total = terms[c * per][...].astype(f32)
        for term in terms[c * per + 1:(c + 1) * per]:
            total = total + term[...].astype(f32)
        buf[:, start - low:end - low] = total.astype(buf.dtype)
    copies = [pltpu.make_async_copy(buf.at[:tokens], ctx_ref.at[:, low:high], sem.at[0])]
    for o in range(opts):
        start = tokens + o * slots
        copies.append(pltpu.make_async_copy(buf.at[start:start + slots], opt_ref.at[o, :, low:high], sem.at[o + 1]))
    for copy in copies:
        copy.start()
    for copy in copies:
        copy.wait()


def final(spans, terms, shapes, before=()):
    flat = sum(terms, [])
    rows, width, opts, n = flat[0].shape[0], spans[-1][1] - spans[0][0], shapes[1].shape[0], len(flat)
    return call(
        functools.partial(final_kernel, spans, len(terms[0])), shapes, [VMEM] * n + [HBM] * len(before),
        rows * width * n, 4 * rows * width * n, out_specs=[HBM, HBM],
        input_output_aliases={n: 0, n + 1: 1} if before else {},
        scratch_shapes=[pltpu.VMEM((rows, width), bf16), pltpu.SemaphoreType.DMA((1 + opts,))],
    )(*flat, *before)


def ring(value, axis, size, shift):
    return lax.ppermute(value, axis, [(i, (i + shift) % size) for i in range(size)])


def swap(value, axis, size, mask):
    return lax.ppermute(value, axis, [(i, i ^ mask) for i in range(size)])


def exclusive(state, axis, size):
    place = lax.axis_index(axis)
    parts, use, windows, step = [], [], [state], 1
    while step < size:
        parts.append(swap(windows[-1], axis, size, step))
        use.append(place & step != 0)
        step *= 2
        if step < size:
            windows.append(add(windows[-1], parts[-1]))
    return parts, use, windows[:2][-1]


def on_device(sizes, q, k, v, oq, ok, ov, offsets, lengths, gain, weight):
    n_seq, n_head, n_sub = sizes
    tokens, feats = q.shape
    opts, slots, _ = oq.shape
    rows = tokens + opts * slots
    heads = feats // DH
    width = weight.shape[1] // (n_head * n_sub)
    head, sub = lax.axis_index("head"), lax.axis_index("sub")

    state = jnp.einsum(
        "thd,the->hde", k.reshape(tokens, heads, DH), v.reshape(tokens, heads, DH), precision=lax.Precision.DEFAULT
    ).astype(bf16)
    parts, use, window = exclusive(state, "seq", n_seq)
    parts = [(part, (0, heads), used) for part, used in zip(parts, use)]

    base, qh, ql, gains = call(
        base_kernel, [Shape((rows, feats), t) for t in (f32, bf16, bf16, f32)], [SMEM] * 2 + [VMEM] * 7 + [ANY],
        12 * rows * rows * feats, 16 * rows * feats,
    )(offsets, lengths, gain[None], q, k, v, oq, ok, ov, window)
    use = jnp.broadcast_to(jnp.stack([p[2] for p in parts]).astype(f32)[:, None], (len(parts), DH))
    normed = call(
        functools.partial(normed_kernel, [p[1] for p in parts]), Shape((rows, feats), bf16),
        [VMEM] * (5 + len(parts)), 6 * rows * DH * feats, 10 * rows * feats,
    )(use, qh, ql, base, gains, *[p[0] for p in parts])

    def blocks(d):
        at = [((head + d) % n_head * n_sub + (sub + s) % n_sub) * width for s in range(n_sub)]
        return [lax.dynamic_slice_in_dim(later, x, width, 1) for x in at]

    def summed(d, spans):
        ours, *theirs = weights[d]
        theirs = [project(normed, w, spans, bf16) for w in theirs]
        ours = project(normed, ours, spans, f32)
        theirs = [[ring(x, "sub", n_sub, s + 1) for x in xs] for s, xs in enumerate(theirs)]
        return list(zip(ours, *theirs))

    later, _ = lax.optimization_barrier((weight, state))
    weights = [blocks(d) for d in range(n_head)]
    spans = [(width * a // 4, width * b // 4) for a, b in SPANS]
    received = {}
    for d in range(1, n_head):
        for span, terms in zip(spans, summed(d, spans)):
            received[d, span] = ring(add(*terms), "head", n_head, d)
    own = dict(zip(spans, summed(0, spans)))
    shapes = (Shape((tokens, width), bf16), Shape((opts, slots, width), bf16))
    out = ()
    for some in (spans[:-1], spans[-1:]):
        terms = [[*own[span]] + [received[d, span] for d in range(1, n_head)] for span in some]
        out = final(some, terms, shapes, out)
    return tuple(out)


def solution(mesh):
    placed = (
        P(("grp", "seq"), ("head", "sub")),
        P(("grp", "seq"), ("head", "sub")),
        P(("grp", "seq"), ("head", "sub")),
        P(("grp", "seq"), None, ("head", "sub")),
        P(("grp", "seq"), None, ("head", "sub")),
        P(("grp", "seq"), None, ("head", "sub")),
        P(("grp", "seq")),
        P(("grp", "seq")),
        P(("head", "sub")),
        P(("head", "sub"), None),
    )
    sizes = tuple(mesh.shape[a] for a in ("seq", "head", "sub"))
    return jax.shard_map(
        functools.partial(on_device, sizes),
        mesh=mesh,
        in_specs=placed,
        out_specs=(P(("grp", "seq"), ("head", "sub")), P(("grp", "seq"), None, ("head", "sub"))),
        check_vma=False,
    )
```

```python
import functools

import jax
import jax.numpy as jnp
from jax import lax
from jax.experimental import pallas as pl
from jax.experimental.pallas import tpu as pltpu
from jax.sharding import PartitionSpec as P

DH = 128
EPS = 1e-05
SPANS = ((0, 2), (2, 3), (3, 4))
OWN_SPANS = ((0, 1), (1, 2), (2, 3), (3, 4))
f32 = jnp.float32
bf16 = jnp.bfloat16
HIGHEST = lax.Precision.HIGHEST
VMEM_LIMIT = 32 * 1024 * 1024

VMEM = pl.BlockSpec(memory_space=pltpu.VMEM)
SMEM = pl.BlockSpec(memory_space=pltpu.SMEM)
HBM = pl.BlockSpec(memory_space=pltpu.HBM)
ANY = pl.BlockSpec(memory_space=pl.ANY)
Shape = jax.ShapeDtypeStruct


def call(body, out_shape, specs, flops, nbytes, out_specs=None, limit=VMEM_LIMIT, **more):
    single = not isinstance(out_shape, (tuple, list))
    if out_specs is None:
        out_specs = VMEM if single else [VMEM] * len(out_shape)
    return pl.pallas_call(
        body,
        out_shape=out_shape,
        in_specs=specs,
        out_specs=out_specs,
        compiler_params=pltpu.CompilerParams(vmem_limit_bytes=limit),
        cost_estimate=pl.CostEstimate(flops=flops, bytes_accessed=nbytes, transcendentals=0),
        **more,
    )


def columns(h):
    return slice(h * DH, (h + 1) * DH)


def dot(a, b, dims):
    return lax.dot_general(a, b, (dims, ((), ())), preferred_element_type=f32)


def base_kernel(
    offsets_ref, lengths_ref, q_ref, k_ref, v_ref, oq_ref, ok_ref, ov_ref, after_ref, out_ref, queries_ref, valid_ref
):
    tokens, (opts, slots, _) = q_ref.shape[0], oq_ref.shape
    rows, most = tokens + opts * slots, opts * slots
    row = lax.broadcasted_iota(jnp.int32, (rows, 1), 0)
    limit, end = row + 1, jnp.full((rows, 1), tokens, jnp.int32)
    for o in range(opts):
        start = tokens + o * slots
        limit = jnp.where(row >= start, offsets_ref[:, o:o + 1], limit)
        end = jnp.where(row >= start, start + lengths_ref[:, o:o + 1], end)
    valid_ref[...] = jnp.broadcast_to((row < end).astype(f32), valid_ref.shape)
    mask = lax.broadcasted_iota(jnp.int32, (rows, tokens), 1) < limit
    i = lax.broadcasted_iota(jnp.int32, (most, most), 0)
    j = lax.broadcasted_iota(jnp.int32, (most, most), 1)
    own = j <= i
    for o in range(1, opts):
        own = own & ((i < o * slots) | (j >= o * slots))
    for h in range(out_ref.shape[1] // DH):
        cols = columns(h)
        oq, ok, ov = (jnp.concatenate([ref[o, :, cols].astype(bf16) for o in range(opts)]) for ref in (oq_ref, ok_ref, ov_ref))
        q = jnp.concatenate([q_ref[:, cols].astype(bf16), oq])
        queries_ref[:, cols] = q
        scores = jnp.where(mask, dot(q, k_ref[:, cols].astype(bf16), ((1,), (1,))), 0.0).astype(bf16)
        own_scores = jnp.where(own, dot(oq, ok, ((1,), (1,))), 0.0).astype(bf16)
        out = dot(scores, v_ref[:, cols].astype(bf16), ((1,), (0,)))
        out_ref[:tokens, cols] = out[:tokens]
        out_ref[tokens:, cols] = out[tokens:] + dot(own_scores, ov, ((1,), (0,)))


def add_kernel(*refs):
    out_ref = refs[-1]
    total = refs[0][:out_ref.shape[0]].astype(f32)
    for ref in refs[1:-1]:
        total = total + ref[:out_ref.shape[0]].astype(f32)
    out_ref[...] = total.astype(out_ref.dtype)


def add(*terms, rows=None):
    shape = (rows or terms[0].shape[0],) + terms[0].shape[1:]
    return call(
        add_kernel, Shape(shape, bf16), [VMEM] * len(terms), len(terms) * terms[0].size, 6 * len(terms) * terms[0].size,
    )(*terms)


def normed_kernel(spans, use_ref, valid_ref, gain_ref, queries_ref, base_ref, *rest):
    parts, out_ref = rest[:-1], rest[-1]
    for h in range(out_ref.shape[1] // DH):
        prefix = jnp.zeros((DH, DH), f32)
        for n, (low, high) in enumerate(spans):
            if low <= h < high:
                prefix = prefix + jnp.where(use_ref[n:n + 1] > 0.0, parts[n][h - low].astype(f32), 0.0)
        cols = columns(h)
        out = base_ref[:, cols] + dot(queries_ref[:, cols], prefix.astype(bf16), ((1,), (0,)))
        scale = lax.rsqrt(jnp.mean(out * out, axis=1, keepdims=True) + EPS)
        out_ref[:, cols] = (out * (scale * valid_ref[...]) * gain_ref[:, cols]).astype(out_ref.dtype)


def project_kernel(spans, rows_ref, weight_ref, *outs):
    for (start, end), out in zip(spans, outs):
        out[...] = jnp.dot(rows_ref[...], weight_ref[:, start:end], preferred_element_type=f32).astype(out.dtype)


def project(rows, weight, spans, dtype):
    count, (depth, width) = rows.shape[0], weight.shape
    return call(
        functools.partial(project_kernel, spans), [Shape((count, b - a), dtype) for a, b in spans], [VMEM] * 2,
        2 * count * depth * width, 2 * depth * (count + width) + 4 * count * width,
    )(rows, weight)


def final_kernel(spans, counts, starts, n_before, *rest):
    terms, (ctx_ref, opt_ref, buf, sem) = rest[:len(starts)], rest[-4:]
    tokens, (opts, slots, _) = ctx_ref.shape[0], opt_ref.shape
    low, high = spans[0][0], spans[-1][1]
    flat = iter(zip(terms, starts))
    for (at, end), count in zip(spans, counts):
        total = 0.0
        for term, start in [next(flat) for _ in range(count)]:
            total = total + term[:, start:start + end - at].astype(f32)
        buf[:, at - low:end - low] = total.astype(buf.dtype)
    copies = [pltpu.make_async_copy(buf.at[:tokens], ctx_ref.at[:, low:high], sem.at[0])]
    for o in range(opts):
        start = tokens + o * slots
        copies.append(pltpu.make_async_copy(buf.at[start:start + slots], opt_ref.at[o, :, low:high], sem.at[o + 1]))
    for copy in copies:
        copy.start()
    for copy in copies:
        copy.wait()


def final(spans, terms, shapes, before=()):
    flat, starts = zip(*sum(terms, []))
    rows, width, opts, n = flat[0].shape[0], spans[-1][1] - spans[0][0], shapes[1].shape[0], len(flat)
    return call(
        functools.partial(final_kernel, spans, [len(some) for some in terms], starts, len(before)), shapes,
        [VMEM] * n + [HBM] * len(before),
        rows * width * n, 4 * rows * width * n, out_specs=[HBM, HBM],
        input_output_aliases={n: 0, n + 1: 1} if before else {},
        scratch_shapes=[pltpu.VMEM((rows, width), bf16), pltpu.SemaphoreType.DMA((1 + opts,))],
    )(*flat, *before)


def ring(value, axis, size, shift):
    return lax.ppermute(value, axis, [(i, (i + shift) % size) for i in range(size)])


def swap(value, axis, size, mask):
    return lax.ppermute(value, axis, [(i, i ^ mask) for i in range(size)])


def upward(value, axis, size, mask):
    return lax.ppermute(value, axis, [(i, i ^ mask) for i in range(size) if not i & mask])


def exclusive(state, axis, size):
    place = lax.axis_index(axis)
    parts, use, windows, step = [], [], [state], 1
    while step < size:
        send = upward if 2 * step == size else swap
        parts.append(send(windows[-1], axis, size, step))
        use.append(place & step != 0)
        step *= 2
        if step < size:
            windows.append(add(windows[-1], parts[-1]))
    return parts, use, windows[:2][-1]


def on_device(sizes, q, k, v, oq, ok, ov, offsets, lengths, gain, weight):
    n_seq, n_head, n_sub = sizes
    tokens, feats = q.shape
    opts, slots, _ = oq.shape
    rows = tokens + opts * slots
    heads = feats // DH
    width = weight.shape[1] // (n_head * n_sub)
    head, sub = lax.axis_index("head"), lax.axis_index("sub")

    state = lax.cond(
        lax.axis_index("seq") < n_seq - 1,
        lambda: jnp.einsum(
            "thd,the->hde", k.reshape(tokens, heads, DH), v.reshape(tokens, heads, DH), precision=lax.Precision.DEFAULT
        ).astype(bf16),
        lambda: jnp.zeros((heads, DH, DH), bf16),
    )
    parts, use, window = exclusive(state, "seq", n_seq)
    parts = [(part, (0, heads), used) for part, used in zip(parts, use)]

    base, queries, valid = call(
        base_kernel, [Shape((rows, feats), f32), Shape((rows, feats), bf16), Shape((rows, DH), f32)], [VMEM] * 8 + [ANY],
        4 * rows * rows * feats, 16 * rows * feats,
    )(offsets[None], lengths[None], q, k, v, oq, ok, ov, window)
    use = jnp.broadcast_to(jnp.stack([p[2] for p in parts]).astype(f32)[:, None], (len(parts), DH))
    normed = call(
        functools.partial(normed_kernel, [p[1] for p in parts]), Shape((rows, feats), bf16),
        [VMEM] * (5 + len(parts)), 2 * rows * DH * feats, 10 * rows * feats,
    )(use, valid, gain[None], queries, base, *[p[0] for p in parts])

    def blocks(d):
        at = [((head + d) % n_head * n_sub + (sub + s) % n_sub) * width for s in range(n_sub)]
        return [lax.dynamic_slice_in_dim(later, x, width, 1) for x in at]

    def summed(d, spans, first=0):
        ours, *theirs = weights[d]
        some = [spans for spans in (spans[:first], spans[first:]) if spans]
        theirs = [sum([list(project(normed, w, spans, bf16)) for spans in some], []) for w in theirs]
        ours = sum([list(project(normed, ours, spans, f32)) for spans in some], [])
        theirs = [[ring(x, "sub", n_sub, s + 1) for x in xs] for s, xs in enumerate(theirs)]
        return list(zip(ours, *theirs))

    later, _ = lax.optimization_barrier((weight, state))
    weights = [blocks(d) for d in range(n_head)]
    spans, own_spans = ([(width * a // 4, width * b // 4) for a, b in some] for some in (SPANS, OWN_SPANS))
    received = []
    for d in range(1, n_head):
        for (low, high), terms in zip(spans, summed(d, spans, 1)):
            received.append((low, high, ring(add(*terms), "head", n_head, d)))
    own = summed(0, own_spans)
    shapes = (Shape((tokens, width), bf16), Shape((opts, slots, width), bf16))
    out, last = (), spans[-1][0]
    for some in ([span for span in own_spans if span[1] <= last], [span for span in own_spans if span[0] >= last]):
        if some:
            terms = [
                [(x, 0) for x in own[own_spans.index(span)]]
                + [(x, span[0] - low) for low, high, x in received if low <= span[0] and span[1] <= high]
                for span in some
            ]
            out = final(some, terms, shapes, out)
    return tuple(out)


def solution(mesh):
    placed = (
        P(("grp", "seq"), ("head", "sub")),
        P(("grp", "seq"), ("head", "sub")),
        P(("grp", "seq"), ("head", "sub")),
        P(("grp", "seq"), None, ("head", "sub")),
        P(("grp", "seq"), None, ("head", "sub")),
        P(("grp", "seq"), None, ("head", "sub")),
        P(("grp", "seq")),
        P(("grp", "seq")),
        P(("head", "sub")),
        P(("head", "sub"), None),
    )
    sizes = tuple(mesh.shape[a] for a in ("seq", "head", "sub"))
    return jax.shard_map(
        functools.partial(on_device, sizes),
        mesh=mesh,
        in_specs=placed,
        out_specs=(P(("grp", "seq"), ("head", "sub")), P(("grp", "seq"), None, ("head", "sub"))),
        check_vma=False,
    )
```

```python
import functools

import jax
import jax.numpy as jnp
from jax import lax
from jax.experimental import pallas as pl
from jax.experimental.pallas import tpu as pltpu
from jax.sharding import PartitionSpec as P

DH = 128
EPS = 1e-05
SPANS = ((0, 4), (4, 6), (6, 8))
OWN_SPANS = ((0, 2), (2, 4), (4, 6), (6, 8))
f32 = jnp.float32
bf16 = jnp.bfloat16
HIGHEST = lax.Precision.HIGHEST
VMEM_LIMIT = 32 * 1024 * 1024

VMEM = pl.BlockSpec(memory_space=pltpu.VMEM)
SMEM = pl.BlockSpec(memory_space=pltpu.SMEM)
HBM = pl.BlockSpec(memory_space=pltpu.HBM)
ANY = pl.BlockSpec(memory_space=pl.ANY)
Shape = jax.ShapeDtypeStruct


def call(body, out_shape, specs, flops, nbytes, out_specs=None, limit=VMEM_LIMIT, **more):
    single = not isinstance(out_shape, (tuple, list))
    if out_specs is None:
        out_specs = VMEM if single else [VMEM] * len(out_shape)
    return pl.pallas_call(
        body,
        out_shape=out_shape,
        in_specs=specs,
        out_specs=out_specs,
        compiler_params=pltpu.CompilerParams(vmem_limit_bytes=limit),
        cost_estimate=pl.CostEstimate(flops=flops, bytes_accessed=nbytes, transcendentals=0),
        **more,
    )


def columns(h):
    return slice(h * DH, (h + 1) * DH)


def dot(a, b, dims):
    return lax.dot_general(a, b, (dims, ((), ())), preferred_element_type=f32)


def base_kernel(
    offsets_ref, lengths_ref, q_ref, k_ref, v_ref, oq_ref, ok_ref, ov_ref, after_ref, use_ref, out_ref, queries_ref, valid_ref
):
    tokens, (opts, slots, _) = q_ref.shape[0], oq_ref.shape
    rows, most = tokens + opts * slots, opts * slots
    row = lax.broadcasted_iota(jnp.int32, (rows, 1), 0)
    limit, end = row + 1, jnp.full((rows, 1), tokens, jnp.int32)
    for o in range(opts):
        start = tokens + o * slots
        limit = jnp.where(row >= start, offsets_ref[:, o:o + 1], limit)
        end = jnp.where(row >= start, start + lengths_ref[:, o:o + 1], end)
    valid_ref[...] = jnp.broadcast_to((row < end).astype(f32), valid_ref.shape)
    mask = lax.broadcasted_iota(jnp.int32, (rows, tokens), 1) < limit
    i = lax.broadcasted_iota(jnp.int32, (most, most), 0)
    j = lax.broadcasted_iota(jnp.int32, (most, most), 1)
    own = j <= i
    for o in range(1, opts):
        own = own & ((i < o * slots) | (j >= o * slots))
    for h in range(out_ref.shape[1] // DH):
        cols = columns(h)
        oq, ok, ov = (jnp.concatenate([ref[o, :, cols].astype(bf16) for o in range(opts)]) for ref in (oq_ref, ok_ref, ov_ref))
        q = jnp.concatenate([q_ref[:, cols].astype(bf16), oq])
        queries_ref[:, cols] = q
        scores = jnp.where(mask, dot(q, k_ref[:, cols].astype(bf16), ((1,), (1,))), 0.0).astype(bf16)
        own_scores = jnp.where(own, dot(oq, ok, ((1,), (1,))), 0.0).astype(bf16)
        out = dot(scores, v_ref[:, cols].astype(bf16), ((1,), (0,)))
        out_ref[:tokens, cols] = out[:tokens]
        out_ref[tokens:, cols] = out[tokens:] + dot(own_scores, ov, ((1,), (0,)))


def add_kernel(*refs):
    out_ref = refs[-1]
    total = refs[0][...].astype(f32)
    for ref in refs[1:-1]:
        total = total + ref[...].astype(f32)
    out_ref[...] = total.astype(out_ref.dtype)


def add(*terms):
    return call(
        add_kernel, Shape(terms[0].shape, bf16), [VMEM] * len(terms),
        len(terms) * terms[0].size, 6 * len(terms) * terms[0].size,
    )(*terms)


def halves_kernel(a_ref, b_ref, first_ref, second_ref):
    total = a_ref[...].astype(f32) + b_ref[...].astype(f32)
    cut = first_ref.shape[0]
    first_ref[...] = total[:cut].astype(first_ref.dtype)
    second_ref[...] = total[cut:].astype(second_ref.dtype)


def add_halves(a, b, cut):
    count, *rest = a.shape
    return call(
        halves_kernel, [Shape((n, *rest), bf16) for n in (cut, count - cut)], [VMEM] * 2, 2 * a.size, 8 * a.size
    )(a, b)


def normed_kernel(spans, use_ref, valid_ref, gain_ref, queries_ref, base_ref, *rest):
    parts, out_ref, prefix_ref = rest[:-2], rest[-2], rest[-1]
    for n, ((low, high), part) in enumerate(zip(spans, parts)):
        part = jnp.where(use_ref[n:n + 1] > 0.0, part[...].astype(f32), 0.0)
        if n:
            part = part + prefix_ref[low:high]
        prefix_ref[low:high] = part
    for h in range(out_ref.shape[1] // DH):
        cols = columns(h)
        out = base_ref[:, cols] + dot(queries_ref[:, cols], prefix_ref[cols].astype(bf16), ((1,), (0,)))
        scale = lax.rsqrt(jnp.mean(out * out, axis=1, keepdims=True) + EPS)
        out_ref[:, cols] = (out * (scale * valid_ref[...]) * gain_ref[:, cols]).astype(out_ref.dtype)


def project_kernel(spans, rows_ref, weight_ref, *outs):
    for (start, end), out in zip(spans, outs):
        out[...] = jnp.dot(rows_ref[...], weight_ref[:, start:end], preferred_element_type=f32).astype(out.dtype)


def project(rows, weight, spans, dtype):
    count, (depth, width) = rows.shape[0], weight.shape
    return call(
        functools.partial(project_kernel, spans), [Shape((count, b - a), dtype) for a, b in spans], [VMEM] * 2,
        2 * count * depth * width, 2 * depth * (count + width) + 4 * count * width,
    )(rows, weight)


def final_kernel(spans, counts, starts, n_before, *rest):
    terms, (ctx_ref, opt_ref, buf, sem) = rest[:len(starts)], rest[-4:]
    tokens, (opts, slots, _) = ctx_ref.shape[0], opt_ref.shape
    low, high = spans[0][0], spans[-1][1]
    flat = iter(zip(terms, starts))
    for (at, end), count in zip(spans, counts):
        total = 0.0
        for term, start in [next(flat) for _ in range(count)]:
            total = total + term[:, start:start + end - at].astype(f32)
        buf[:, at - low:end - low] = total.astype(buf.dtype)
    copies = [pltpu.make_async_copy(buf.at[:tokens], ctx_ref.at[:, low:high], sem.at[0])]
    for o in range(opts):
        start = tokens + o * slots
        copies.append(pltpu.make_async_copy(buf.at[start:start + slots], opt_ref.at[o, :, low:high], sem.at[o + 1]))
    for copy in copies:
        copy.start()
    for copy in copies:
        copy.wait()


def final(spans, terms, shapes, before=()):
    flat, starts = zip(*sum(terms, []))
    rows, width, opts, n = flat[0].shape[0], spans[-1][1] - spans[0][0], shapes[1].shape[0], len(flat)
    return call(
        functools.partial(final_kernel, spans, [len(some) for some in terms], starts, len(before)), shapes,
        [VMEM] * n + [HBM] * len(before),
        rows * width * n, 4 * rows * width * n, out_specs=[HBM, HBM],
        input_output_aliases={n: 0, n + 1: 1} if before else {},
        scratch_shapes=[pltpu.VMEM((rows, width), bf16), pltpu.SemaphoreType.DMA((1 + opts,))],
    )(*flat, *before)


def ring(value, axis, size, shift):
    return lax.ppermute(value, axis, [(i, (i + shift) % size) for i in range(size)])


def swap(value, axis, size, mask):
    return lax.ppermute(value, axis, [(i, i ^ mask) for i in range(size)])


def upward(value, axis, size, mask):
    return lax.ppermute(value, axis, [(i, i ^ mask) for i in range(size) if not i & mask])


def exclusive(state, axis, size):
    count, place = state.shape[0], lax.axis_index(axis)
    parts, sent, step = [], state, 1
    while step < size:
        used = place & step != 0
        if step > 1 and 2 * step == size:
            cut = count * 15 // 32 // 16 * 16
            pieces = add_halves(window[0], window[1], cut)
            parts += [
                (swap(pieces[0], axis, size, step), (0, cut), used), (upward(pieces[1], axis, size, step), (cut, count), used)
            ]
            sent = pieces[0] if step == 2 else sent
        else:
            total = state if step == 1 else add(*window)
            sent = total if step == 2 else sent
            parts.append((swap(total, axis, size, step), (0, count), used))
            window = (total, parts[-1][0])
        step *= 2
    return parts, sent


def on_device(sizes, q, k, v, oq, ok, ov, offsets, lengths, gain, weight):
    n_seq, n_head, n_sub = sizes
    tokens, feats = q.shape
    opts, slots, _ = oq.shape
    rows = tokens + opts * slots
    heads = feats // DH
    width = weight.shape[1] // (n_head * n_sub)
    head, sub = lax.axis_index("head"), lax.axis_index("sub")

    state = lax.cond(
        lax.axis_index("seq") < n_seq - 1,
        lambda: jnp.einsum(
            "thd,the->hde", k.reshape(tokens, heads, DH), v.reshape(tokens, heads, DH), precision=lax.Precision.DEFAULT
        ).astype(bf16).reshape(feats, DH),
        lambda: jnp.zeros((feats, DH), bf16),
    )
    parts, window = exclusive(state, "seq", n_seq)

    use = jnp.broadcast_to(jnp.stack([p[2] for p in parts]).astype(f32)[:, None], (len(parts), DH))
    base, queries, valid = call(
        base_kernel, [Shape((rows, feats), f32), Shape((rows, feats), bf16), Shape((rows, DH), f32)], [VMEM] * 8 + [ANY] * 2,
        4 * rows * rows * feats, 16 * rows * feats,
    )(offsets[None], lengths[None], q, k, v, oq, ok, ov, window, use)
    normed = call(
        functools.partial(normed_kernel, [p[1] for p in parts]), Shape((rows, feats), bf16),
        [VMEM] * (5 + len(parts)), 2 * rows * DH * feats, 10 * rows * feats,
        scratch_shapes=[pltpu.VMEM((feats, DH), f32)],
    )(use, valid, gain[None], queries, base, *[p[0] for p in parts])

    def blocks(d):
        at = [((head + d) % n_head * n_sub + (sub + s) % n_sub) * width for s in range(n_sub)]
        return [lax.dynamic_slice_in_dim(later, x, width, 1) for x in at]

    def summed(d, spans, first=0):
        ours, *theirs = weights[d]
        some = [spans for spans in (spans[:first], spans[first:]) if spans]
        theirs = [sum([list(project(normed, w, spans, bf16)) for spans in some], []) for w in theirs]
        ours = sum([list(project(normed, ours, spans, f32)) for spans in some], [])
        theirs = [[ring(x, "sub", n_sub, s + 1) for x in xs] for s, xs in enumerate(theirs)]
        return list(zip(ours, *theirs))

    later, _ = lax.optimization_barrier((weight, state))
    weights = [blocks(d) for d in range(n_head)]
    spans, own_spans = ([(width * a // 8, width * b // 8) for a, b in some] for some in (SPANS, OWN_SPANS))
    parts = []
    for d in range(1, n_head):
        for span, terms in zip(spans, summed(d, spans, 1)):
            parts.append((*span, ring(add(*terms), "head", n_head, d)))
    for span, terms in zip(own_spans, summed(0, own_spans)):
        parts += [(*span, x) for x in terms]
    cuts = sorted({low for low, _, _ in parts} | {width})
    steps, last = list(zip(cuts, cuts[1:])), spans[-1][0]
    shapes, out = (Shape((tokens, width), bf16), Shape((opts, slots, width), bf16)), ()
    for some in ([step for step in steps if step[1] <= last], [step for step in steps if step[0] >= last]):
        if some:
            terms = [[(x, at - low) for low, high, x in parts if low <= at and end <= high] for at, end in some]
            out = final(some, terms, shapes, out)
    return tuple(out)


def solution(mesh):
    placed = (
        P(("grp", "seq"), ("head", "sub")),
        P(("grp", "seq"), ("head", "sub")),
        P(("grp", "seq"), ("head", "sub")),
        P(("grp", "seq"), None, ("head", "sub")),
        P(("grp", "seq"), None, ("head", "sub")),
        P(("grp", "seq"), None, ("head", "sub")),
        P(("grp", "seq")),
        P(("grp", "seq")),
        P(("head", "sub")),
        P(("head", "sub"), None),
    )
    sizes = tuple(mesh.shape[a] for a in ("seq", "head", "sub"))
    return jax.shard_map(
        functools.partial(on_device, sizes),
        mesh=mesh,
        in_specs=placed,
        out_specs=(P(("grp", "seq"), ("head", "sub")), P(("grp", "seq"), None, ("head", "sub"))),
        check_vma=False,
    )
```

```python
import functools

import jax
import jax.numpy as jnp
from jax import lax
from jax.experimental import pallas as pl
from jax.experimental.pallas import tpu as pltpu
from jax.sharding import PartitionSpec as P

DH = 128
EPS = 1e-05
SPANS = ((0, 4), (4, 6), (6, 8))
OWN_SPANS = ((0, 2), (2, 4), (4, 6), (6, 8))
f32 = jnp.float32
bf16 = jnp.bfloat16
HIGHEST = lax.Precision.HIGHEST
VMEM_LIMIT = 32 * 1024 * 1024

VMEM = pl.BlockSpec(memory_space=pltpu.VMEM)
SMEM = pl.BlockSpec(memory_space=pltpu.SMEM)
HBM = pl.BlockSpec(memory_space=pltpu.HBM)
ANY = pl.BlockSpec(memory_space=pl.ANY)
Shape = jax.ShapeDtypeStruct


def call(body, out_shape, specs, flops, nbytes, out_specs=None, limit=VMEM_LIMIT, **more):
    single = not isinstance(out_shape, (tuple, list))
    if out_specs is None:
        out_specs = VMEM if single else [VMEM] * len(out_shape)
    return pl.pallas_call(
        body,
        out_shape=out_shape,
        in_specs=specs,
        out_specs=out_specs,
        compiler_params=pltpu.CompilerParams(vmem_limit_bytes=limit),
        cost_estimate=pl.CostEstimate(flops=flops, bytes_accessed=nbytes, transcendentals=0),
        **more,
    )


def columns(h):
    return slice(h * DH, (h + 1) * DH)


def dot(a, b, dims):
    return lax.dot_general(a, b, (dims, ((), ())), preferred_element_type=f32)


def base_kernel(
    offsets_ref, lengths_ref, q_ref, k_ref, v_ref, oq_ref, ok_ref, ov_ref, after_ref, use_ref, out_ref, queries_ref, valid_ref
):
    tokens, (opts, slots, _) = q_ref.shape[0], oq_ref.shape
    rows, most = tokens + opts * slots, opts * slots
    row = lax.broadcasted_iota(jnp.int32, (rows, 1), 0)
    limit, end = row + 1, jnp.full((rows, 1), tokens, jnp.int32)
    for o in range(opts):
        start = tokens + o * slots
        limit = jnp.where(row >= start, offsets_ref[:, o:o + 1], limit)
        end = jnp.where(row >= start, start + lengths_ref[:, o:o + 1], end)
    valid_ref[...] = jnp.broadcast_to((row < end).astype(f32), valid_ref.shape)
    mask = lax.broadcasted_iota(jnp.int32, (rows, tokens), 1) < limit
    i = lax.broadcasted_iota(jnp.int32, (most, most), 0)
    j = lax.broadcasted_iota(jnp.int32, (most, most), 1)
    own = j <= i
    for o in range(1, opts):
        own = own & ((i < o * slots) | (j >= o * slots))
    for h in range(out_ref.shape[1] // DH):
        cols = columns(h)
        oq, ok, ov = (jnp.concatenate([ref[o, :, cols].astype(bf16) for o in range(opts)]) for ref in (oq_ref, ok_ref, ov_ref))
        q = jnp.concatenate([q_ref[:, cols].astype(bf16), oq])
        queries_ref[:, cols] = q
        scores = jnp.where(mask, dot(q, k_ref[:, cols].astype(bf16), ((1,), (1,))), 0.0).astype(bf16)
        own_scores = jnp.where(own, dot(oq, ok, ((1,), (1,))), 0.0).astype(bf16)
        out = dot(scores, v_ref[:, cols].astype(bf16), ((1,), (0,)))
        out_ref[:tokens, cols] = out[:tokens]
        out_ref[tokens:, cols] = out[tokens:] + dot(own_scores, ov, ((1,), (0,)))


def add_kernel(*refs):
    out_ref = refs[-1]
    total = refs[0][...].astype(f32)
    for ref in refs[1:-1]:
        total = total + ref[...].astype(f32)
    out_ref[...] = total.astype(out_ref.dtype)


def add(*terms):
    return call(
        add_kernel, Shape(terms[0].shape, bf16), [VMEM] * len(terms),
        len(terms) * terms[0].size, 6 * len(terms) * terms[0].size,
    )(*terms)


def split_kernel(x_ref, *outs):
    at = 0
    for out in outs:
        out[...] = x_ref[at:at + out.shape[0]]
        at += out.shape[0]


def split(x, spans):
    shapes = [Shape((high - low, *x.shape[1:]), x.dtype) for low, high in spans]
    return call(split_kernel, shapes, [VMEM], 0, 4 * x.size)(x)


def normed_kernel(spans, width, after, use_ref, valid_ref, gain_ref, queries_ref, base_ref, *rest):
    parts, prefix_ref, outs = rest[:len(spans)], rest[-1], rest[len(spans) + after:-1]
    weights, out_ref, firsts = outs[:len(outs) // 2], outs[len(outs) // 2], outs[len(outs) // 2 + 1:]
    for n, ((low, high), part) in enumerate(zip(spans, parts)):
        part = jnp.where(use_ref[n:n + 1] > 0.0, part[...].astype(f32), 0.0)
        if n > 1:
            part = part + prefix_ref[low:high]
        prefix_ref[low:high] = part
    for h in range(out_ref.shape[1] // DH):
        cols = columns(h)
        out = base_ref[:, cols] + dot(queries_ref[:, cols], prefix_ref[cols].astype(bf16), ((1,), (0,)))
        scale = lax.rsqrt(jnp.mean(out * out, axis=1, keepdims=True) + EPS)
        out_ref[:, cols] = (out * (scale * valid_ref[...]) * gain_ref[:, cols]).astype(out_ref.dtype)
    for weight, first in zip(weights, firsts):
        first[...] = jnp.dot(out_ref[...], weight[:, :width], preferred_element_type=f32).astype(first.dtype)


def project_kernel(spans, rows_ref, weight_ref, *outs):
    for (start, end), out in zip(spans, outs):
        out[...] = jnp.dot(rows_ref[...], weight_ref[:, start:end], preferred_element_type=f32).astype(out.dtype)


def project(rows, weight, spans, dtype):
    count, (depth, width) = rows.shape[0], weight.shape
    return call(
        functools.partial(project_kernel, spans), [Shape((count, b - a), dtype) for a, b in spans], [VMEM] * 2,
        2 * count * depth * width, 2 * depth * (count + width) + 4 * count * width,
    )(rows, weight)


def final_kernel(spans, counts, starts, n_before, *rest):
    terms, (ctx_ref, opt_ref, buf, sem) = rest[:len(starts)], rest[-4:]
    tokens, (opts, slots, _) = ctx_ref.shape[0], opt_ref.shape
    low, high = spans[0][0], spans[-1][1]
    flat = iter(zip(terms, starts))
    for (at, end), count in zip(spans, counts):
        total = 0.0
        for term, start in [next(flat) for _ in range(count)]:
            total = total + term[:, start:start + end - at].astype(f32)
        buf[:, at - low:end - low] = total.astype(buf.dtype)
    copies = [pltpu.make_async_copy(buf.at[:tokens], ctx_ref.at[:, low:high], sem.at[0])]
    for o in range(opts):
        start = tokens + o * slots
        copies.append(pltpu.make_async_copy(buf.at[start:start + slots], opt_ref.at[o, :, low:high], sem.at[o + 1]))
    for copy in copies:
        copy.start()
    for copy in copies:
        copy.wait()


def final(spans, terms, shapes, before=()):
    flat, starts = zip(*sum(terms, []))
    rows, width, opts, n = flat[0].shape[0], spans[-1][1] - spans[0][0], shapes[1].shape[0], len(flat)
    return call(
        functools.partial(final_kernel, spans, [len(some) for some in terms], starts, len(before)), shapes,
        [VMEM] * n + [HBM] * len(before),
        rows * width * n, 4 * rows * width * n, out_specs=[HBM, HBM],
        input_output_aliases={n: 0, n + 1: 1} if before else {},
        scratch_shapes=[pltpu.VMEM((rows, width), bf16), pltpu.SemaphoreType.DMA((1 + opts,))],
    )(*flat, *before)


def ring(value, axis, size, shift):
    return lax.ppermute(value, axis, [(i, (i + shift) % size) for i in range(size)])


def swap(value, axis, size, mask):
    return lax.ppermute(value, axis, [(i, i ^ mask) for i in range(size)])


def upward(value, axis, size, mask):
    return lax.ppermute(value, axis, [(i, i ^ mask) for i in range(size) if not i & mask])


def exclusive(state, axis, size):
    count, place = state.shape[0], lax.axis_index(axis)
    cut = count * 15 // 32 // 16 * 16
    spans = [(0, cut), (cut, count)]
    windows, parts, step = split(state, spans), [], 1
    while step < size:
        sends = [swap, upward if step > 1 and 2 * step == size else swap]
        got = [send(x, axis, size, step) for send, x in zip(sends, windows)]
        parts += [(x, span, place & step != 0) for x, span in zip(got, spans)]
        step *= 2
        if step < size:
            windows = [add(x, y) for x, y in zip(windows, got)]
    return parts, windows[1]


def on_device(sizes, q, k, v, oq, ok, ov, offsets, lengths, gain, weight):
    n_seq, n_head, n_sub = sizes
    tokens, feats = q.shape
    opts, slots, _ = oq.shape
    rows = tokens + opts * slots
    heads = feats // DH
    width = weight.shape[1] // (n_head * n_sub)
    head, sub = lax.axis_index("head"), lax.axis_index("sub")

    state = lax.cond(
        lax.axis_index("seq") < n_seq - 1,
        lambda: jnp.einsum(
            "thd,the->hde", k.reshape(tokens, heads, DH), v.reshape(tokens, heads, DH), precision=lax.Precision.DEFAULT
        ).astype(bf16).reshape(feats, DH),
        lambda: jnp.zeros((feats, DH), bf16),
    )
    parts, window = exclusive(state, "seq", n_seq)

    use = jnp.broadcast_to(jnp.stack([p[2] for p in parts]).astype(f32)[:, None], (len(parts), DH))
    base, queries, valid = call(
        base_kernel, [Shape((rows, feats), f32), Shape((rows, feats), bf16), Shape((rows, DH), f32)], [VMEM] * 8 + [ANY] * 2,
        4 * rows * rows * feats, 16 * rows * feats,
    )(offsets[None], lengths[None], q, k, v, oq, ok, ov, window, use)
    def blocks(d, after):
        later, _ = lax.optimization_barrier((weight, after))
        at = [((head + d) % n_head * n_sub + (sub + s) % n_sub) * width for s in range(n_sub)]
        return [lax.dynamic_slice_in_dim(later, x, width, 1) for x in at]

    weights = [blocks(d, state if d else base) for d in range(n_head)]
    spans, own_spans = ([(width * a // 8, width * b // 8) for a, b in some] for some in (SPANS, OWN_SPANS))
    first, early = spans[0][1], weights[1][1:] if n_head > 1 else []
    normed, *firsts = call(
        functools.partial(normed_kernel, [p[1] for p in parts], first, n_sub),
        [Shape((rows, feats), bf16)] + [Shape((rows, first), bf16)] * len(early),
        [VMEM] * (5 + len(parts)) + [ANY] * n_sub + [VMEM] * len(early),
        2 * rows * DH * feats, 10 * rows * feats, scratch_shapes=[pltpu.VMEM((feats, DH), f32)],
    )(use, valid, gain[None], queries, base, *[p[0] for p in parts], *weights[0], *early)

    def summed(d, spans, done=()):
        ours, *theirs = weights[d]
        some = [spans for spans in (spans[:1], spans[1:]) if spans] if d == 1 else [spans]
        theirs = [
            list(early) + sum([list(project(normed, w, spans, bf16)) for spans in some[len(early):]], [])
            for w, early in zip(theirs, [[x] for x in done] or [[]] * len(theirs))
        ]
        ours = sum([list(project(normed, ours, spans, f32)) for spans in some], [])
        theirs = [[ring(x, "sub", n_sub, s + 1) for x in xs] for s, xs in enumerate(theirs)]
        return list(zip(ours, *theirs))

    parts = []
    for d in range(1, n_head):
        for span, terms in zip(spans, summed(d, spans, firsts if d == 1 else ())):
            parts.append((*span, ring(add(*terms), "head", n_head, d)))
    for span, terms in zip(own_spans, summed(0, own_spans)):
        parts += [(*span, x) for x in terms]
    cuts = sorted({low for low, _, _ in parts} | {width})
    steps, last = list(zip(cuts, cuts[1:])), spans[-1][0]
    shapes, out = (Shape((tokens, width), bf16), Shape((opts, slots, width), bf16)), ()
    for some in ([step for step in steps if step[1] <= last], [step for step in steps if step[0] >= last]):
        if some:
            terms = [[(x, at - low) for low, high, x in parts if low <= at and end <= high] for at, end in some]
            out = final(some, terms, shapes, out)
    return tuple(out)


def solution(mesh):
    placed = (
        P(("grp", "seq"), ("head", "sub")),
        P(("grp", "seq"), ("head", "sub")),
        P(("grp", "seq"), ("head", "sub")),
        P(("grp", "seq"), None, ("head", "sub")),
        P(("grp", "seq"), None, ("head", "sub")),
        P(("grp", "seq"), None, ("head", "sub")),
        P(("grp", "seq")),
        P(("grp", "seq")),
        P(("head", "sub")),
        P(("head", "sub"), None),
    )
    sizes = tuple(mesh.shape[a] for a in ("seq", "head", "sub"))
    return jax.shard_map(
        functools.partial(on_device, sizes),
        mesh=mesh,
        in_specs=placed,
        out_specs=(P(("grp", "seq"), ("head", "sub")), P(("grp", "seq"), None, ("head", "sub"))),
        check_vma=False,
    )
```

```python
import functools

import jax
import jax.numpy as jnp
from jax import lax
from jax.experimental import pallas as pl
from jax.experimental.pallas import tpu as pltpu
from jax.sharding import PartitionSpec as P

DH = 128
EPS = 1e-05
SPANS = ((0, 4), (4, 6), (6, 8))
OWN_SPANS = ((0, 2), (2, 4), (4, 6), (6, 8))
f32 = jnp.float32
bf16 = jnp.bfloat16
HIGHEST = lax.Precision.HIGHEST
VMEM_LIMIT = 32 * 1024 * 1024

VMEM = pl.BlockSpec(memory_space=pltpu.VMEM)
SMEM = pl.BlockSpec(memory_space=pltpu.SMEM)
HBM = pl.BlockSpec(memory_space=pltpu.HBM)
ANY = pl.BlockSpec(memory_space=pl.ANY)
Shape = jax.ShapeDtypeStruct


def call(body, out_shape, specs, flops, nbytes, out_specs=None, limit=VMEM_LIMIT, **more):
    single = not isinstance(out_shape, (tuple, list))
    if out_specs is None:
        out_specs = VMEM if single else [VMEM] * len(out_shape)
    return pl.pallas_call(
        body,
        out_shape=out_shape,
        in_specs=specs,
        out_specs=out_specs,
        compiler_params=pltpu.CompilerParams(vmem_limit_bytes=limit),
        cost_estimate=pl.CostEstimate(flops=flops, bytes_accessed=nbytes, transcendentals=0),
        **more,
    )


def columns(h):
    return slice(h * DH, (h + 1) * DH)


def dot(a, b, dims):
    return lax.dot_general(a, b, (dims, ((), ())), preferred_element_type=f32)


def base_kernel(
    offsets_ref, lengths_ref, q_ref, k_ref, v_ref, oq_ref, ok_ref, ov_ref, after_ref, use_ref, out_ref, queries_ref, valid_ref
):
    tokens, (opts, slots, _) = q_ref.shape[0], oq_ref.shape
    rows, most = tokens + opts * slots, opts * slots
    row = lax.broadcasted_iota(jnp.int32, (rows, 1), 0)
    limit, end = row + 1, jnp.full((rows, 1), tokens, jnp.int32)
    for o in range(opts):
        start = tokens + o * slots
        limit = jnp.where(row >= start, offsets_ref[:, o:o + 1], limit)
        end = jnp.where(row >= start, start + lengths_ref[:, o:o + 1], end)
    valid_ref[...] = jnp.broadcast_to((row < end).astype(f32), valid_ref.shape)
    mask = lax.broadcasted_iota(jnp.int32, (rows, tokens), 1) < limit
    i = lax.broadcasted_iota(jnp.int32, (most, most), 0)
    j = lax.broadcasted_iota(jnp.int32, (most, most), 1)
    own = j <= i
    for o in range(1, opts):
        own = own & ((i < o * slots) | (j >= o * slots))
    for h in range(out_ref.shape[1] // DH):
        cols = columns(h)
        oq, ok, ov = (jnp.concatenate([ref[o, :, cols].astype(bf16) for o in range(opts)]) for ref in (oq_ref, ok_ref, ov_ref))
        q = jnp.concatenate([q_ref[:, cols].astype(bf16), oq])
        queries_ref[:, cols] = q
        scores = jnp.where(mask, dot(q, k_ref[:, cols].astype(bf16), ((1,), (1,))), 0.0).astype(bf16)
        own_scores = jnp.where(own, dot(oq, ok, ((1,), (1,))), 0.0).astype(bf16)
        out = dot(scores, v_ref[:, cols].astype(bf16), ((1,), (0,)))
        out_ref[:tokens, cols] = out[:tokens]
        out_ref[tokens:, cols] = out[tokens:] + dot(own_scores, ov, ((1,), (0,)))


def add_kernel(*refs):
    out_ref = refs[-1]
    total = refs[0][...].astype(f32)
    for ref in refs[1:-1]:
        total = total + ref[...].astype(f32)
    out_ref[...] = total.astype(out_ref.dtype)


def add(*terms):
    return call(
        add_kernel, Shape(terms[0].shape, bf16), [VMEM] * len(terms),
        len(terms) * terms[0].size, 6 * len(terms) * terms[0].size,
    )(*terms)


def split_kernel(x_ref, *outs):
    at = 0
    for out in outs:
        out[...] = x_ref[at:at + out.shape[0]]
        at += out.shape[0]


def split(x, spans):
    shapes = [Shape((high - low, *x.shape[1:]), x.dtype) for low, high in spans]
    return call(split_kernel, shapes, [VMEM], 0, 4 * x.size)(x)


def normed_kernel(spans, width, after, use_ref, valid_ref, gain_ref, queries_ref, base_ref, *rest):
    parts, prefix_ref, outs = rest[:len(spans)], rest[-1], rest[len(spans) + after:-1]
    weights, out_ref, firsts = outs[:len(outs) // 2], outs[len(outs) // 2], outs[len(outs) // 2 + 1:]
    for n, ((low, high), part) in enumerate(zip(spans, parts)):
        part = jnp.where(use_ref[n:n + 1] > 0.0, part[...].astype(f32), 0.0)
        if n > 1:
            part = part + prefix_ref[low:high]
        prefix_ref[low:high] = part
    for h in range(out_ref.shape[1] // DH):
        cols = columns(h)
        out = base_ref[:, cols] + dot(queries_ref[:, cols], prefix_ref[cols].astype(bf16), ((1,), (0,)))
        scale = lax.rsqrt(jnp.mean(out * out, axis=1, keepdims=True) + EPS)
        out_ref[:, cols] = (out * (scale * valid_ref[...]) * gain_ref[:, cols]).astype(out_ref.dtype)
    for weight, first in zip(weights, firsts):
        first[...] = jnp.dot(out_ref[...], weight[:, :width], preferred_element_type=f32).astype(first.dtype)


def project_kernel(spans, rows_ref, weight_ref, *outs):
    for (start, end), out in zip(spans, outs):
        out[...] = jnp.dot(rows_ref[...], weight_ref[:, start:end], preferred_element_type=f32).astype(out.dtype)


def project(rows, weight, spans, dtype):
    count, (depth, width) = rows.shape[0], weight.shape
    return call(
        functools.partial(project_kernel, spans), [Shape((count, b - a), dtype) for a, b in spans], [VMEM] * 2,
        2 * count * depth * width, 2 * depth * (count + width) + 4 * count * width,
    )(rows, weight)


def final_kernel(spans, counts, starts, n_before, *rest):
    terms, (ctx_ref, opt_ref, buf, sem) = rest[:len(starts)], rest[-4:]
    tokens, (opts, slots, _) = ctx_ref.shape[0], opt_ref.shape
    low, high = spans[0][0], spans[-1][1]
    flat = iter(zip(terms, starts))
    for (at, end), count in zip(spans, counts):
        total = 0.0
        for term, start in [next(flat) for _ in range(count)]:
            total = total + term[:, start:start + end - at].astype(f32)
        buf[:, at - low:end - low] = total.astype(buf.dtype)
    copies = [pltpu.make_async_copy(buf.at[:tokens], ctx_ref.at[:, low:high], sem.at[0])]
    for o in range(opts):
        start = tokens + o * slots
        copies.append(pltpu.make_async_copy(buf.at[start:start + slots], opt_ref.at[o, :, low:high], sem.at[o + 1]))
    for copy in copies:
        copy.start()
    for copy in copies:
        copy.wait()


def final(spans, terms, shapes, before=()):
    flat, starts = zip(*sum(terms, []))
    rows, width, opts, n = flat[0].shape[0], spans[-1][1] - spans[0][0], shapes[1].shape[0], len(flat)
    return call(
        functools.partial(final_kernel, spans, [len(some) for some in terms], starts, len(before)), shapes,
        [VMEM] * n + [HBM] * len(before),
        rows * width * n, 4 * rows * width * n, out_specs=[HBM, HBM],
        input_output_aliases={n: 0, n + 1: 1} if before else {},
        scratch_shapes=[pltpu.VMEM((rows, width), bf16), pltpu.SemaphoreType.DMA((1 + opts,))],
    )(*flat, *before)


def ring(value, axis, size, shift):
    return lax.ppermute(value, axis, [(i, (i + shift) % size) for i in range(size)])


def swap(value, axis, size, mask):
    return lax.ppermute(value, axis, [(i, i ^ mask) for i in range(size)])


def upward(value, axis, size, mask):
    return lax.ppermute(value, axis, [(i, i ^ mask) for i in range(size) if not i & mask])


def exclusive(state, axis, size):
    count, place = state.shape[0], lax.axis_index(axis)
    cut = count * 15 // 32 // 16 * 16
    spans = [(0, cut), (cut, count)]
    windows, parts, step = split(state, spans), [], 1
    while step < size:
        sends = [swap, upward if step > 1 and 2 * step == size else swap]
        got = [send(x, axis, size, step) for send, x in zip(sends, windows)]
        parts += [(x, span, place & step != 0) for x, span in zip(got, spans)]
        step *= 2
        if step < size:
            windows = [add(x, y) for x, y in zip(windows, got)]
    return parts, windows[1]


def on_device(sizes, q, k, v, oq, ok, ov, offsets, lengths, gain, weight):
    n_seq, n_head, n_sub = sizes
    tokens, feats = q.shape
    opts, slots, _ = oq.shape
    rows = tokens + opts * slots
    heads = feats // DH
    width = weight.shape[1] // (n_head * n_sub)
    head, sub = lax.axis_index("head"), lax.axis_index("sub")

    state = lax.cond(
        lax.axis_index("seq") < n_seq - 1,
        lambda: jnp.einsum(
            "thd,the->hde", k.reshape(tokens, heads, DH), v.reshape(tokens, heads, DH), precision=lax.Precision.DEFAULT
        ).astype(bf16).reshape(feats, DH),
        lambda: jnp.zeros((feats, DH), bf16),
    )
    parts, window = exclusive(state, "seq", n_seq)

    use = jnp.broadcast_to(jnp.stack([p[2] for p in parts]).astype(f32)[:, None], (len(parts), DH))
    base, queries, valid = call(
        base_kernel, [Shape((rows, feats), f32), Shape((rows, feats), bf16), Shape((rows, DH), f32)], [VMEM] * 8 + [ANY] * 2,
        4 * rows * rows * feats, 16 * rows * feats,
    )(offsets[None], lengths[None], q, k, v, oq, ok, ov, window, use)
    def blocks(d, after):
        later, _ = lax.optimization_barrier((weight, after))
        at = [((head + d) % n_head * n_sub + (sub + s) % n_sub) * width for s in range(n_sub)]
        return [lax.dynamic_slice_in_dim(later, x, width, 1) for x in at]

    weights = [blocks(d, state if d else base) for d in range(n_head)]
    spans, own_spans = ([(width * a // 8, width * b // 8) for a, b in some] for some in (SPANS, OWN_SPANS))
    first, early = spans[0][1], weights[1][1:] if n_head > 1 else []
    normed, *firsts = call(
        functools.partial(normed_kernel, [p[1] for p in parts], first, n_sub),
        [Shape((rows, feats), bf16)] + [Shape((rows, first), bf16)] * len(early),
        [VMEM] * (5 + len(parts)) + [ANY] * n_sub + [VMEM] * len(early),
        2 * rows * DH * feats, 10 * rows * feats, scratch_shapes=[pltpu.VMEM((feats, DH), f32)],
    )(use, valid, gain[None], queries, base, *[p[0] for p in parts], *weights[0], *early)

    def summed(d, spans, done=()):
        (ours, *theirs), rows = weights[d], normed
        some = [spans for spans in (spans[:1], spans[1:]) if spans] if d == 1 else [spans]
        mine = list(project(rows, ours, some[0], f32))
        if done:
            rows, _ = lax.optimization_barrier((normed, mine))
        theirs = [
            list(early) + sum([list(project(rows, w, spans, bf16)) for spans in some[len(early):]], [])
            for w, early in zip(theirs, [[x] for x in done] or [[]] * len(theirs))
        ]
        mine += sum([list(project(normed, ours, spans, f32)) for spans in some[1:]], [])
        theirs = [[ring(x, "sub", n_sub, s + 1) for x in xs] for s, xs in enumerate(theirs)]
        return list(zip(mine, *theirs))

    parts = []
    for d in range(1, n_head):
        for span, terms in zip(spans, summed(d, spans, firsts if d == 1 else ())):
            parts.append((*span, ring(add(*terms), "head", n_head, d)))
    for span, terms in zip(own_spans, summed(0, own_spans)):
        parts += [(*span, x) for x in terms]
    cuts = sorted({low for low, _, _ in parts} | {width})
    steps, last = list(zip(cuts, cuts[1:])), spans[-1][0]
    shapes, out = (Shape((tokens, width), bf16), Shape((opts, slots, width), bf16)), ()
    for some in ([step for step in steps if step[1] <= last], [step for step in steps if step[0] >= last]):
        if some:
            terms = [[(x, at - low) for low, high, x in parts if low <= at and end <= high] for at, end in some]
            out = final(some, terms, shapes, out)
    return tuple(out)


def solution(mesh):
    placed = (
        P(("grp", "seq"), ("head", "sub")),
        P(("grp", "seq"), ("head", "sub")),
        P(("grp", "seq"), ("head", "sub")),
        P(("grp", "seq"), None, ("head", "sub")),
        P(("grp", "seq"), None, ("head", "sub")),
        P(("grp", "seq"), None, ("head", "sub")),
        P(("grp", "seq")),
        P(("grp", "seq")),
        P(("head", "sub")),
        P(("head", "sub"), None),
    )
    sizes = tuple(mesh.shape[a] for a in ("seq", "head", "sub"))
    return jax.shard_map(
        functools.partial(on_device, sizes),
        mesh=mesh,
        in_specs=placed,
        out_specs=(P(("grp", "seq"), ("head", "sub")), P(("grp", "seq"), None, ("head", "sub"))),
        check_vma=False,
    )
```
